32 devices in a mesh: query: 2 (over x), ckpt: 2 (over core), mp: 8 (over z, y).
Axes of the slice: x: 2, y: 2, z: 4, core: 2. Of those that a mesh axis runs over, the one named last changes fastest.
Arguments:
- activations: bfloat16 [2, 1280, 5120], P('ckpt', 'query', 'mp'), parts along dimension 1, may hold values from -6 to 6
- cotangents: bfloat16 [2, 1280, 5120], P('ckpt', 'query', 'mp'), parts along dimension 1, may hold values from -6 to 6
- w_in: bfloat16 [2, 5120, 20480], P('ckpt', None, 'mp'), may hold values from -0.078125 to 0.078125
- b_in: bfloat16 [2, 20480], P('ckpt', 'mp'), may hold values from -3 to 3
- w_out: bfloat16 [2, 20480, 5120], P('ckpt', 'mp'), may hold values from -0.0390625 to 0.0390625
- rates: float32 [2], P('ckpt'), may hold values from 0.5 to 2
- proj_in: bfloat16 [64, 5120], P(None, 'mp'), may hold values from -0.078125 to 0.078125
- proj_out: bfloat16 [20480, 64], P('mp'), may hold values from -0.0390625 to 0.0390625
- lengths: int32 [80], P('query'), parts along dimension 0, may hold values from 1 to 16, 400 in all
Outputs:
- influence: float32 [64, 8], P(('query', 'mp')), parts along dimension 0
The draws below stay inside these ranges and needn't reach their ends.
There are 2 independent parts, one for each index of `query`. The reference program is written for one: setup_inputs(seed, part) draws one part's arguments, and reference() takes and returns one part's arrays. A program takes and returns all parts, laid end to end along the dimension named above; an argument that names none is the same for every part. Nothing has to cross between parts.
Inputs may be any that keep to these rules, and one draw needn't show every extreme that they name: The lengths of one part sum to exactly 400; some example has exactly 16.
All inputs are finite; a program needn't handle non-finite values.
Results may differ from the reference program's by a relative error of at most 0.0042.
Values may be sent and summed in bfloat16 or wider, within the bound.
A program may use at most 192 MiB of HBM per device.

```python
import math
import jax
import jax.numpy as jnp
import numpy as np
from jax import lax

D = 5120
FF = 20480
K_IN = 64
K_OUT = 64
NTR = 32
NTE = 8
SEQ = 16
CKPT = 2
TOK = 640
LIVE = 400


def level_of(rng, dims, cuts, least, largest):
    level = 1.0
    for dim, blocks in cuts:
        draws = jax.random.uniform(jax.random.fold_in(jax.random.fold_in(rng, 6), dim), (blocks,), jnp.float32, least / len(cuts), largest / len(cuts))
        level = level * jnp.repeat(jnp.exp(draws), dims[dim] // blocks).reshape((-1,) + (1,) * (len(dims) - 1 - dim))
    return level


def profile(amount, total, reach, slope):
    portions = [(1 << 20) // math.isqrt(grade ** slope) + 1 for grade in range(2, amount + 1)]
    surplus, holding = total - reach - (amount - 1), [1] * (amount - 1)
    while surplus > 0:
        free = [i for i in range(amount - 1) if holding[i] < reach]
        mass, remaining = sum([portions[i] for i in free]), surplus
        for i in free:
            more = min(reach - holding[i], max(1, remaining * portions[i] // mass), surplus)
            holding[i] = holding[i] + more
            surplus = surplus - more
    return np.array([reach] + holding)


def uneven(stream_key, amount, total, limit, slope):
    if amount == 2:
        one = jax.random.randint(stream_key, (), max(1, total - limit), min(limit, total - 1) + 1)
        return jnp.stack([one, total - one])
    tallies = jnp.asarray(profile(amount, total, limit, slope), jnp.int32)
    pairs = (amount - 1) // 2
    giver, receiver = tallies[1:1 + 2 * pairs:2], tallies[2:2 + 2 * pairs:2]
    slack = jnp.minimum(giver - 1, limit - receiver)
    shifted = jax.random.randint(jax.random.fold_in(stream_key, 1), (pairs,), 0, 1 << 20) % (slack + 1)
    tallies = tallies.at[1:1 + 2 * pairs:2].set(giver - shifted).at[2:2 + 2 * pairs:2].set(receiver + shifted)
    return tallies[jax.random.permutation(jax.random.fold_in(stream_key, 2), amount)]


def scatter_about(rng, extent, width, reach, cuts=(), held_as=jnp.bfloat16):
    values = width * jax.random.normal(rng, extent, jnp.float32)
    if cuts:
        values = values * level_of(rng, extent, cuts, -0.22, 0.18)
    return jnp.clip(values, -reach, reach).astype(held_as)


def setup_inputs(seed: int = 0, part: int = 0) -> dict:
    keys = jax.random.split(jax.random.key(seed), 10)
    own_keys = jax.random.split(jax.random.fold_in(keys[9], part), 10)
    activations = scatter_about(own_keys[0], (CKPT, TOK, D), 1.0, 6.0, ((0, 2), (2, 8)))
    cotangents = scatter_about(own_keys[1], (CKPT, TOK, D), 1.0, 6.0, ((0, 2), (2, 8)))
    w_in = scatter_about(keys[2], (CKPT, D, FF), D ** -0.5, 0.078125, ((0, 2), (2, 8)))
    b_in = scatter_about(keys[3], (CKPT, FF), 0.5, 3.0, ((0, 2), (1, 8)))
    w_out = scatter_about(keys[4], (CKPT, FF, D), FF ** -0.5, 0.0390625, ((0, 2), (1, 8)))
    rates = jnp.clip(jnp.exp(math.log(2.0) - 1.3862944 * jax.random.uniform(keys[5], (CKPT,), jnp.float32) ** level_of(keys[5], (CKPT,), ((0, 2),), -0.2, 0.2)), 0.5, 2.0)
    proj_in = scatter_about(keys[6], (K_IN, D), D ** -0.5, 0.078125, ((1, 8),))
    proj_out = scatter_about(keys[7], (FF, K_OUT), FF ** -0.5, 0.0390625, ((0, 8),))
    lengths = uneven(own_keys[8], NTR + NTE, LIVE, SEQ, 1).astype(jnp.int32)
    return {"activations": activations, "cotangents": cotangents, "w_in": w_in, "b_in": b_in, "w_out": w_out, "rates": rates, "proj_in": proj_in, "proj_out": proj_out, "lengths": lengths}


def gelu_slope(z):
    return 0.5 * (1.0 + jax.scipy.special.erf(z / math.sqrt(2.0))) + z * jnp.exp(-0.5 * z * z) / math.sqrt(2.0 * math.pi)

def reference(activations, cotangents, w_in, b_in, w_out, rates, proj_in, proj_out, lengths):
    examples = lengths.shape[0]
    tok = activations.shape[1]
    seq = tok // examples
    k_in = proj_in.shape[0]
    k_out = proj_out.shape[1]
    row_ids = jnp.arange(tok, dtype=jnp.int32)
    owner = row_ids // seq
    live = (row_ids % seq < jnp.take(lengths, owner)).astype(jnp.float32)
    total = jnp.zeros((NTR, NTE), jnp.float32)
    for check in range(activations.shape[0]):
        inputs = activations[check]
        pre = jnp.dot(inputs, w_in[check], preferred_element_type=jnp.float32) + b_in[check].astype(jnp.float32)
        back = lax.dot_general(cotangents[check], w_out[check], (((1,), (1,)), ((), ())), preferred_element_type=jnp.float32)
        dpre = (back * gelu_slope(pre)).astype(jnp.bfloat16)
        left = lax.dot_general(inputs, proj_in, (((1,), (1,)), ((), ())), preferred_element_type=jnp.float32) * live[:, None]
        right = jnp.dot(dpre, proj_out, preferred_element_type=jnp.float32)
        grads = jnp.einsum('esi,esj->eij', left.reshape(examples, seq, k_in), right.reshape(examples, seq, k_out), precision=lax.Precision.HIGHEST)
        grads = grads.reshape(examples, k_in * k_out)
        tile = jnp.dot(grads[:NTR], grads[NTR:].T, precision=lax.Precision.HIGHEST)
        total = total + rates[check] / math.sqrt(k_in * k_out) * tile
    return total
```

```python
import functools
import math

import jax
import jax.numpy as jnp
from jax import lax
from jax.experimental import pallas as pl
from jax.experimental.pallas import tpu as pltpu
from jax.sharding import PartitionSpec as P

NTR = 32
LIVE = 400


def gelu_slope(z):
    return 0.5 * (1.0 + jax.scipy.special.erf(z / math.sqrt(2.0))) + z * jnp.exp(
        -0.5 * z * z
    ) / math.sqrt(2.0 * math.pi)


def body(activations, cotangents, w_in, b_in, w_out, rates, proj_in, proj_out, lengths):
    x_local = activations[0]
    dy_local = cotangents[0]
    w_first = w_in[0]
    w_second = w_out[0]
    bias = b_in[0]
    rate = rates[0]
    examples = lengths.shape[0]
    padded_rows = x_local.shape[0]
    seq = padded_rows // examples
    k_in = proj_in.shape[0]
    k_out = proj_out.shape[1]
    columns = jnp.arange(examples, dtype=jnp.int32)
    ends = jnp.cumsum(lengths)
    starts = ends - lengths
    row_ids = jnp.arange(LIVE, dtype=jnp.int32)
    owner = jnp.sum((row_ids[:, None] >= ends[None, :]).astype(jnp.int32), axis=1)
    belongs = owner[:, None] == columns[None, :]
    start_of = jnp.sum(jnp.where(belongs, starts[None, :], 0), axis=1)
    source = owner * seq + row_ids - start_of
    x_rows = jnp.take(x_local, source, axis=0)
    dy_rows = jnp.take(dy_local, source, axis=0)
    live = jnp.ones((LIVE,), jnp.float32)

    def to_slots(values):
        slots = jnp.zeros((padded_rows, values.shape[1]), jnp.float32).at[source].set(values)
        return slots.reshape(examples, seq, values.shape[1])

    x_piece = lax.all_gather(x_rows, "mp", axis=1, tiled=True)
    map_piece = lax.all_gather(proj_in, "mp", axis=1, tiled=True)
    pre_acc = jnp.dot(x_piece, w_first, preferred_element_type=jnp.float32)
    left_acc = lax.dot_general(
        x_piece, map_piece, (((1,), (1,)), ((), ())), preferred_element_type=jnp.float32
    )
    pre = pre_acc
    left = left_acc
    pre = pre + bias.astype(jnp.float32)
    back = lax.dot_general(
        lax.all_gather(dy_rows, "mp", axis=1, tiled=True),
        w_second,
        (((1,), (1,)), ((), ())),
        preferred_element_type=jnp.float32,
    )
    dpre = (back * gelu_slope(pre)).astype(jnp.bfloat16)
    left = left * live[:, None]
    right = jnp.dot(dpre, proj_out, preferred_element_type=jnp.float32)
    factor = rate / math.sqrt(k_in * k_out)
    left_blocks = to_slots(left)
    right_blocks = to_slots(right)
    grads = jnp.einsum("esi,esj->ije", left_blocks, right_blocks, precision=lax.Precision.HIGHEST)
    grads = grads.reshape(k_in * k_out, examples)
    owned = lax.psum_scatter(grads, "mp", scatter_dimension=0, tiled=True)
    partial_tile = (
        lax.dot_general(
            owned[:, :NTR],
            owned[:, NTR:],
            (((0,), (0,)), ((), ())),
            precision=lax.Precision.HIGHEST,
        )
        * factor
    )
    tile = lax.psum_scatter(partial_tile, "mp", scatter_dimension=0, tiled=True)
    return lax.psum(tile, "ckpt")


PIECES = (
    ((0, 1), (1, 1), (0, 0), (2, 1), (2, 0), (3, 1), (3, 0), (1, 0)),
    ((1, 1), (2, 1), (1, 0), (0, 1), (3, 1), (0, 0), (2, 0), (3, 0)),
)
INWARD, OUTWARD, ACROSS = 0, 1, 2
TILE = 512
SHARE = 16
HIGH = lax.Precision.HIGHEST


def routes(rank, owner, same, part):
    out = []
    if same:
        if owner <= rank:
            out.append(INWARD)
        if rank == 1 and owner >= 1:
            out.append(OUTWARD)
        if rank == 0 and not (owner == 1 and part == 1):
            out.append(ACROSS)
        if rank == 1 and owner != 0:
            out.append(ACROSS)
    elif rank == 0 and owner == 0:
        out.append(INWARD)
    return out


def fused_kernel(
    x_ref, dy_ref, w_in, bias_ref, w_out, rate_ref, map_ref, proj_ref, len_ref,
    out_ref,
    xs, dys, win_buf, wout_buf, pre, back, maps, right, gram, parts_out, parts_in, tile_out, tile_in,
    send_sem, recv_sem, w_sem, map_send, map_recv, part_send, part_recv, tile_send, tile_recv,
):
    f32, bf16 = jnp.float32, jnp.bfloat16
    me = lax.axis_index("mp")
    q = lax.axis_index("query")
    c = lax.axis_index("ckpt")
    z = me // 2
    y = me % 2
    far = z // 2
    rank = z + far * (3 - 2 * z)
    group = q * 2 + c
    width = x_ref.shape[2]
    hidden = w_in.shape[2]
    tiles = hidden // TILE
    examples = len_ref.shape[1]
    padded = x_ref.shape[1]
    seq = padded // examples
    k_in = map_ref.shape[0]
    k_out = proj_ref.shape[1]
    stacks = (xs, dys)
    cuts = (((0, 208), (208, 208)), ((0, 208), (208, 192)))

    barrier = pltpu.get_barrier_semaphore()
    for d in range(16):
        for dc in range(2):
            if d < 8 and (d or dc):
                pl.semaphore_signal(
                    barrier, inc=1,
                    device_id={"mp": (me + d) % 8, "ckpt": (c + dc) % 2},
                    device_id_type=pl.DeviceIdType.MESH,
                )
    for dc in range(2):
        pl.semaphore_signal(
            barrier, inc=1,
            device_id={"query": 1 - q, "ckpt": (c + dc) % 2},
            device_id_type=pl.DeviceIdType.MESH,
        )

    def index_of(owner, same):
        zz = owner + far * (3 - 2 * owner)
        return zz * 2 + (y + 1 - same) % 2

    def piece(k):
        (o0, s0), (o1, s1) = PIECES[0][k], PIECES[1][k]
        return index_of(o0 + rank * (o1 - o0), s0 + rank * (s1 - s0))

    def weights(array, k):
        slot = (array * 8 + k) % 3
        at = pl.multiple_of(piece(k) * width, 128)
        if array == 0:
            return pltpu.make_async_copy(
                w_in.at[0, pl.ds(at, width), :], win_buf.at[slot], w_sem.at[array, slot]
            )
        return pltpu.make_async_copy(
            w_out.at[0, :, pl.ds(at, width)], wout_buf.at[slot], w_sem.at[array, slot]
        )

    for k in range(2):
        weights(0, k).start()

    lens = jnp.broadcast_to(len_ref[...].astype(f32), (8, examples)).astype(bf16)

    def spans(count, example_of):
        e = lax.broadcasted_iota(jnp.int32, (examples, count), 0)
        t = example_of(lax.broadcasted_iota(jnp.int32, (examples, count), 1))
        start = jnp.dot(lens, (e < t).astype(f32).astype(bf16), preferred_element_type=f32)
        size = jnp.dot(lens, (e == t).astype(f32).astype(bf16), preferred_element_type=f32)
        return start[0:1], size[0:1]

    start, size = spans(padded, lambda t: t // seq)
    place = (lax.broadcasted_iota(jnp.int32, (1, padded), 1) % seq).astype(f32)
    target = jnp.where(place < size, start + place, -1.0)
    rows = lax.broadcasted_iota(jnp.int32, (LIVE, padded), 0).astype(f32)
    pick = jnp.where(rows == target, 1.0, 0.0).astype(bf16)
    xs[me, 0:LIVE, :] = jnp.dot(pick, x_ref[0], preferred_element_type=f32).astype(bf16)
    xs[me, LIVE : LIVE + SHARE, :] = map_ref[pl.ds(pl.multiple_of(group * SHARE, SHARE), SHARE), :]

    pl.semaphore_wait(barrier, 17)

    sgn = 1 - 2 * far
    targets = ((z + sgn) * 2 + y, (z - sgn) * 2 + y, z * 2 + 1 - y)

    def copy(array, k, part, direction):
        o = piece(k)
        first, count = cuts[array][part]
        there = stacks[array].at[o, pl.ds(first, count), :]
        return pltpu.make_async_remote_copy(
            src_ref=there,
            dst_ref=there,
            send_sem=send_sem.at[array, k, part, direction],
            recv_sem=recv_sem.at[array, o, part],
            device_id={"mp": targets[direction]},
            device_id_type=pl.DeviceIdType.MESH,
        )

    def each_route(array, k, do):
        for part in range(2):
            for direction in (OUTWARD, INWARD, ACROSS):
                ranks = [r for r in range(2) if direction in routes(r, *PIECES[r][k], part)]
                if len(ranks) == 2:
                    do(array, k, part, direction)
                elif ranks:
                    pl.when(rank == ranks[0])(functools.partial(do, array, k, part, direction))
        if k == 4:
            pl.when(rank == 1)(functools.partial(do, array, 2, 1, OUTWARD))

    def send(array, k, part, direction):
        copy(array, k, part, direction).start()

    def sent(array, k, part, direction):
        copy(array, k, part, direction).wait_send()

    def arrived(array, k):
        for part in range(2):
            copy(array, k, part, ACROSS).wait_recv()

    each_route(0, 0, send)
    dys[me] = jnp.dot(pick, dy_ref[0], preferred_element_type=f32).astype(bf16)

    def accumulate(array, k):
        o = piece(k)
        slot = (array * 8 + k) % 3

        @pl.loop(0, tiles)
        def _(t):
            cols = pl.ds(pl.multiple_of(t * TILE, TILE), TILE)
            if array == 0:
                term = jnp.dot(xs[o, 0:LIVE, :], win_buf[slot, :, cols], preferred_element_type=f32)
                if k == 0:
                    pre[:, cols] = term + bias_ref[:, cols].astype(f32)
                else:
                    pre[:, cols] += term
            else:
                term = lax.dot_general(
                    dys[o], wout_buf[slot, cols, :], (((1,), (1,)), ((), ())), preferred_element_type=f32
                )
                if k == 0:
                    back[:, cols] = term
                elif k < 7:
                    back[:, cols] += term
                else:
                    dpre = ((back[:, cols] + term) * pre[:, cols]).astype(bf16)
                    part = jnp.dot(dpre, proj_ref[cols, :], preferred_element_type=f32)
                    right[...] += part

    for array in range(2):
        for k in range(8):
            if array == 0 and k == 6:
                each_route(1, 0, send)
            if k > 0:
                arrived(array, k)
                each_route(array, k, send)
            if array == 0 and k == 7:
                own = maps.at[group]
                for peer in range(1, 4):
                    pltpu.make_async_remote_copy(
                        src_ref=xs.at[:, pl.ds(LIVE, SHARE), :],
                        dst_ref=own,
                        send_sem=map_send.at[peer],
                        recv_sem=map_recv.at[peer],
                        device_id={"query": (q + peer // 2) % 2, "ckpt": (c + peer % 2) % 2},
                        device_id_type=pl.DeviceIdType.MESH,
                    ).start()
                maps[group] = xs[:, LIVE : LIVE + SHARE, :]
            ahead = array * 8 + k + 2
            if ahead < 16:
                weights(ahead // 8, ahead % 8).start()
            weights(array, k).wait()
            accumulate(array, k)
            if array == 1 and k < tiles:
                cols = pl.ds(k * TILE, TILE)
                pre[:, cols] = gelu_slope_tile(pre[:, cols])
            if array == 1 and k == 5:
                right[...] = jnp.zeros_like(right)
                for peer in range(1, 4):
                    other = ((q + peer // 2) % 2) * 2 + (c + peer % 2) % 2
                    pltpu.make_async_remote_copy(
                        src_ref=xs.at[:, pl.ds(LIVE, SHARE), :],
                        dst_ref=maps.at[other],
                        send_sem=map_send.at[peer],
                        recv_sem=map_recv.at[peer],
                        device_id={"query": (q + peer // 2) % 2, "ckpt": (c + peer % 2) % 2},
                        device_id_type=pl.DeviceIdType.MESH,
                    ).wait()
                left = jnp.zeros((LIVE, k_in), f32)
                for o in range(8):
                    left += lax.dot_general(
                        xs[o, 0:LIVE, :],
                        maps[:, o].reshape(k_in, width),
                        (((1,), (1,)), ((), ())),
                        preferred_element_type=f32,
                    )
                gram[...] = lax.dot_general(
                    left, left, (((1,), (1,)), ((), ())), precision=HIGH, preferred_element_type=f32
                )
                for j in range(8):
                    each_route(0, j, sent)

    token = lax.broadcasted_iota(jnp.int32, (LIVE, 64), 0).astype(f32)
    start, size = spans(64, lambda t: jnp.where(t % 8 < 4, t // 8 * 4 + t % 8, -1))
    train = jnp.where((token >= start) & (token < start + size), 1.0, 0.0)
    token = lax.broadcasted_iota(jnp.int32, (LIVE, 128), 0).astype(f32)
    start, size = spans(128, lambda t: t + NTR)
    test = jnp.where((token >= start) & (token < start + size), 1.0, 0.0)

    parts_out[...] = right[...].T.reshape(8, k_out // 8, LIVE)

    def part_copy(d):
        return pltpu.make_async_remote_copy(
            src_ref=parts_out.at[(me + d) % 8],
            dst_ref=parts_in.at[d],
            send_sem=part_send.at[d],
            recv_sem=part_recv.at[d],
            device_id={"mp": (me + d) % 8},
            device_id_type=pl.DeviceIdType.MESH,
        )

    for d in range(1, 8):
        part_copy(d).start()
    parts_in[0] = parts_out[me]
    for j in range(8):
        each_route(1, j, sent)
    for d in range(1, 8):
        part_copy(d).wait_recv()
    total = jnp.sum(parts_in[...], axis=0)
    both = gram[...] * jnp.dot(total.T, total, precision=HIGH, preferred_element_type=f32)
    half = jnp.dot(both, test, precision=HIGH, preferred_element_type=f32)
    score = jnp.dot(train.T, half, precision=HIGH, preferred_element_type=f32)
    score = score * (rate_ref[0] / math.sqrt(k_in * k_out))
    tile_out[...] = score.reshape(8, 8, 128)

    def tile_copy(d, dc):
        return pltpu.make_async_remote_copy(
            src_ref=tile_out.at[(me + d) % 8],
            dst_ref=tile_in.at[d * 2 + dc],
            send_sem=tile_send.at[d * 2 + dc],
            recv_sem=tile_recv.at[d * 2 + dc],
            device_id={"mp": (me + d) % 8, "ckpt": (c + dc) % 2},
            device_id_type=pl.DeviceIdType.MESH,
        )

    for d in range(8):
        for dc in range(2):
            if d or dc:
                tile_copy(d, dc).start()
    tile_in[0] = tile_out[me]
    for d in range(1, 8):
        part_copy(d).wait_send()
    for d in range(8):
        for dc in range(2):
            if d or dc:
                tile_copy(d, dc).wait()
    out_ref[...] = jnp.sum(tile_in[...], axis=0)[0:4, 0:8]


def gelu_slope_tile(z):
    return 0.5 * (1.0 + lax.erf(z * (1.0 / math.sqrt(2.0)))) + z * jnp.exp(-0.5 * z * z) * (
        1.0 / math.sqrt(2.0 * math.pi)
    )


def fused(activations, cotangents, w_in, b_in, w_out, rates, proj_in, proj_out, lengths):
    width = activations.shape[2]
    hidden = w_in.shape[2]
    k_in = proj_in.shape[0]
    k_out = proj_out.shape[1]
    f32, bf16 = jnp.float32, jnp.bfloat16
    vmem = pl.BlockSpec(memory_space=pltpu.VMEM)
    hbm = pl.BlockSpec(memory_space=pl.ANY)
    smem = pl.BlockSpec(memory_space=pltpu.SMEM)
    dma = pltpu.SemaphoreType.DMA
    return pl.pallas_call(
        fused_kernel,
        out_shape=jax.ShapeDtypeStruct((4, 8), f32),
        in_specs=[vmem, vmem, hbm, vmem, hbm, smem, vmem, vmem, vmem],
        out_specs=vmem,
        scratch_shapes=[
            pltpu.VMEM((8, LIVE + SHARE, width), bf16),
            pltpu.VMEM((8, LIVE, width), bf16),
            pltpu.VMEM((3, width, hidden), bf16),
            pltpu.VMEM((3, hidden, width), bf16),
            pltpu.VMEM((LIVE, hidden), f32),
            pltpu.VMEM((LIVE, hidden), f32),
            pltpu.VMEM((4, 8, SHARE, width), bf16),
            pltpu.VMEM((LIVE, k_out), f32),
            pltpu.VMEM((LIVE, LIVE), f32),
            pltpu.VMEM((8, k_out // 8, LIVE), f32),
            pltpu.VMEM((8, k_out // 8, LIVE), f32),
            pltpu.VMEM((8, 8, 128), f32),
            pltpu.VMEM((16, 8, 128), f32),
            dma((2, 8, 2, 3)),
            dma((2, 8, 2)),
            dma((2, 3)),
            dma((4,)),
            dma((4,)),
            dma((8,)),
            dma((8,)),
            dma((16,)),
            dma((16,)),
        ],
        compiler_params=pltpu.CompilerParams(
            collective_id=0, has_side_effects=True, vmem_limit_bytes=60 * 1024 * 1024
        ),
        cost_estimate=pl.CostEstimate(
            flops=4 * LIVE * 8 * width * hidden,
            bytes_accessed=32 * width * hidden,
            transcendentals=2 * LIVE * hidden,
        ),
        name="influence",
    )(
        activations, cotangents, w_in, b_in, w_out, rates, proj_in, proj_out,
        lengths.reshape(1, lengths.shape[0]),
    )


def solution(mesh):
    placed = (
        P("ckpt", "query", "mp"),
        P("ckpt", "query", "mp"),
        P("ckpt", None, "mp"),
        P("ckpt", "mp"),
        P("ckpt", "mp", None),
        P("ckpt"),
        P(None, "mp"),
        P("mp", None),
        P("query"),
    )
    fits = mesh.shape["mp"] == 8 and mesh.shape["query"] == 2 and mesh.shape["ckpt"] == 2
    return jax.shard_map(
        fused if fits else body,
        mesh=mesh,
        in_specs=placed,
        out_specs=P(("query", "mp"), None),
        check_vma=False,
    )
```

```python
import functools
import math

import jax
import jax.numpy as jnp
from jax import lax
from jax.experimental import pallas as pl
from jax.experimental.pallas import tpu as pltpu
from jax.sharding import PartitionSpec as P

NTR = 32
LIVE = 400


def gelu_slope(z):
    return 0.5 * (1.0 + jax.scipy.special.erf(z / math.sqrt(2.0))) + z * jnp.exp(
        -0.5 * z * z
    ) / math.sqrt(2.0 * math.pi)


def body(activations, cotangents, w_in, b_in, w_out, rates, proj_in, proj_out, lengths):
    x_local = activations[0]
    dy_local = cotangents[0]
    w_first = w_in[0]
    w_second = w_out[0]
    bias = b_in[0]
    rate = rates[0]
    examples = lengths.shape[0]
    padded_rows = x_local.shape[0]
    seq = padded_rows // examples
    k_in = proj_in.shape[0]
    k_out = proj_out.shape[1]
    columns = jnp.arange(examples, dtype=jnp.int32)
    ends = jnp.cumsum(lengths)
    starts = ends - lengths
    row_ids = jnp.arange(LIVE, dtype=jnp.int32)
    owner = jnp.sum((row_ids[:, None] >= ends[None, :]).astype(jnp.int32), axis=1)
    belongs = owner[:, None] == columns[None, :]
    start_of = jnp.sum(jnp.where(belongs, starts[None, :], 0), axis=1)
    source = owner * seq + row_ids - start_of
    x_rows = jnp.take(x_local, source, axis=0)
    dy_rows = jnp.take(dy_local, source, axis=0)
    live = jnp.ones((LIVE,), jnp.float32)

    def to_slots(values):
        slots = jnp.zeros((padded_rows, values.shape[1]), jnp.float32).at[source].set(values)
        return slots.reshape(examples, seq, values.shape[1])

    x_piece = lax.all_gather(x_rows, "mp", axis=1, tiled=True)
    map_piece = lax.all_gather(proj_in, "mp", axis=1, tiled=True)
    pre_acc = jnp.dot(x_piece, w_first, preferred_element_type=jnp.float32)
    left_acc = lax.dot_general(
        x_piece, map_piece, (((1,), (1,)), ((), ())), preferred_element_type=jnp.float32
    )
    pre = pre_acc
    left = left_acc
    pre = pre + bias.astype(jnp.float32)
    back = lax.dot_general(
        lax.all_gather(dy_rows, "mp", axis=1, tiled=True),
        w_second,
        (((1,), (1,)), ((), ())),
        preferred_element_type=jnp.float32,
    )
    dpre = (back * gelu_slope(pre)).astype(jnp.bfloat16)
    left = left * live[:, None]
    right = jnp.dot(dpre, proj_out, preferred_element_type=jnp.float32)
    factor = rate / math.sqrt(k_in * k_out)
    left_blocks = to_slots(left)
    right_blocks = to_slots(right)
    grads = jnp.einsum("esi,esj->ije", left_blocks, right_blocks, precision=lax.Precision.HIGHEST)
    grads = grads.reshape(k_in * k_out, examples)
    owned = lax.psum_scatter(grads, "mp", scatter_dimension=0, tiled=True)
    partial_tile = (
        lax.dot_general(
            owned[:, :NTR],
            owned[:, NTR:],
            (((0,), (0,)), ((), ())),
            precision=lax.Precision.HIGHEST,
        )
        * factor
    )
    tile = lax.psum_scatter(partial_tile, "mp", scatter_dimension=0, tiled=True)
    return lax.psum(tile, "ckpt")


PIECES = (
    ((0, 1), (1, 1), (0, 0), (2, 1), (2, 0), (3, 1), (3, 0), (1, 0)),
    ((1, 1), (2, 1), (1, 0), (0, 1), (3, 1), (0, 0), (2, 0), (3, 0)),
)
INWARD, OUTWARD, ACROSS = 0, 1, 2
TILE = 512
SHARE = 16
HIGH = lax.Precision.HIGHEST
PARTS = 4


def routes(rank, owner, same, part):
    out = []
    if same:
        if owner <= rank:
            out.append(INWARD)
        if rank == 1 and owner >= 1:
            out.append(OUTWARD)
        if rank == 0 and not (owner == 1 and part >= PARTS // 2):
            out.append(ACROSS)
        if rank == 1 and owner != 0:
            out.append(ACROSS)
    elif rank == 0 and owner == 0:
        out.append(INWARD)
    return out


def fused_kernel(
    x_ref, dy_ref, w_in, bias_ref, w_out, rate_ref, map_ref, proj_ref, len_ref,
    out_ref,
    xs, dys, win_buf, wout_buf, pre, back, maps, right, gram, parts_out, parts_in, tile_out, tile_in, dy_buf, proj_buf,
    load_sem, send_sem, recv_sem, w_sem, map_send, map_recv, part_send, part_recv, tile_send, tile_recv,
):
    f32, bf16 = jnp.float32, jnp.bfloat16
    me = lax.axis_index("mp")
    q = lax.axis_index("query")
    c = lax.axis_index("ckpt")
    z = me // 2
    y = me % 2
    far = z // 2
    rank = z + far * (3 - 2 * z)
    group = q * 2 + c
    width = x_ref.shape[2]
    hidden = w_in.shape[2]
    tiles = hidden // TILE
    examples = len_ref.shape[1]
    padded = x_ref.shape[1]
    seq = padded // examples
    k_in = map_ref.shape[0]
    k_out = proj_ref.shape[1]
    stacks = (xs, dys)
    cuts = []
    for stack in stacks:
        blocks = stack.shape[1] // SHARE
        edges = [blocks * p // PARTS * SHARE for p in range(PARTS + 1)]
        cuts.append([(a, b - a) for a, b in zip(edges, edges[1:])])

    barrier = pltpu.get_barrier_semaphore()
    for d in range(16):
        for dc in range(2):
            if d < 8 and (d or dc):
                pl.semaphore_signal(
                    barrier, inc=1,
                    device_id={"mp": (me + d) % 8, "ckpt": (c + dc) % 2},
                    device_id_type=pl.DeviceIdType.MESH,
                )
    for dc in range(2):
        pl.semaphore_signal(
            barrier, inc=1,
            device_id={"query": 1 - q, "ckpt": (c + dc) % 2},
            device_id_type=pl.DeviceIdType.MESH,
        )

    def index_of(owner, same):
        zz = owner + far * (3 - 2 * owner)
        return zz * 2 + (y + 1 - same) % 2

    def piece(k):
        (o0, s0), (o1, s1) = PIECES[0][k], PIECES[1][k]
        return index_of(o0 + rank * (o1 - o0), s0 + rank * (s1 - s0))

    def weights(array, k):
        slot = (array * 8 + k) % 3
        at = pl.multiple_of(piece(k) * width, 128)
        if array == 0:
            return pltpu.make_async_copy(
                w_in.at[0, pl.ds(at, width), :], win_buf.at[slot], w_sem.at[array, slot]
            )
        return pltpu.make_async_copy(
            w_out.at[0, :, pl.ds(at, width)], wout_buf.at[slot], w_sem.at[array, slot]
        )

    dy_load = pltpu.make_async_copy(dy_ref.at[0], dy_buf, load_sem.at[0])
    proj_load = pltpu.make_async_copy(proj_ref, proj_buf, load_sem.at[1])
    dy_load.start()
    proj_load.start()
    for k in range(2):
        weights(0, k).start()

    lens = jnp.broadcast_to(len_ref[...].astype(f32), (8, examples)).astype(bf16)

    def spans(count, example_of):
        e = lax.broadcasted_iota(jnp.int32, (examples, count), 0)
        t = example_of(lax.broadcasted_iota(jnp.int32, (examples, count), 1))
        start = jnp.dot(lens, (e < t).astype(f32).astype(bf16), preferred_element_type=f32)
        size = jnp.dot(lens, (e == t).astype(f32).astype(bf16), preferred_element_type=f32)
        return start[0:1], size[0:1]

    start, size = spans(padded, lambda t: t // seq)
    place = (lax.broadcasted_iota(jnp.int32, (1, padded), 1) % seq).astype(f32)
    target = jnp.where(place < size, start + place, -1.0)
    rows = lax.broadcasted_iota(jnp.int32, (LIVE, padded), 0).astype(f32)
    pick = jnp.where(rows == target, 1.0, 0.0).astype(bf16)
    xs[me, 0:LIVE, :] = jnp.dot(pick, x_ref[0], preferred_element_type=f32).astype(bf16)
    xs[me, LIVE : LIVE + SHARE, :] = map_ref[pl.ds(pl.multiple_of(group * SHARE, SHARE), SHARE), :]

    pl.semaphore_wait(barrier, 17)

    sgn = 1 - 2 * far
    targets = ((z + sgn) * 2 + y, (z - sgn) * 2 + y, z * 2 + 1 - y)

    def copy(array, k, part, direction):
        o = piece(k)
        first, count = cuts[array][part]
        there = stacks[array].at[o, pl.ds(first, count), :]
        return pltpu.make_async_remote_copy(
            src_ref=there,
            dst_ref=there,
            send_sem=send_sem.at[array, k, part, direction],
            recv_sem=recv_sem.at[array, o, part],
            device_id={"mp": targets[direction]},
            device_id_type=pl.DeviceIdType.MESH,
        )

    def each_route(array, k, part, do):
        for direction in (OUTWARD, INWARD, ACROSS):
            ranks = [r for r in range(2) if direction in routes(r, *PIECES[r][k], part)]
            if len(ranks) == 2:
                do(array, k, part, direction)
            elif ranks:
                pl.when(rank == ranks[0])(functools.partial(do, array, k, part, direction))
        if k == 4 and part >= PARTS // 2:
            pl.when(rank == 1)(functools.partial(do, array, 2, part, OUTWARD))

    def send(array, k, part, direction):
        copy(array, k, part, direction).start()

    def sent(array, k, part, direction):
        copy(array, k, part, direction).wait_send()

    def pass_on(array, *ks):
        for part in range(PARTS):
            for k in ks:
                if k > 0:
                    copy(array, k, part, ACROSS).wait_recv()
                each_route(array, k, part, send)

    def all_sent(array):
        for k in range(8):
            for part in range(PARTS):
                each_route(array, k, part, sent)

    pass_on(0, 0)
    dy_load.wait()
    proj_load.wait()
    dys[me] = jnp.dot(pick, dy_buf[...], preferred_element_type=f32).astype(bf16)

    def accumulate(array, k):
        o = piece(k)
        slot = (array * 8 + k) % 3

        @pl.loop(0, tiles)
        def _(t):
            cols = pl.ds(pl.multiple_of(t * TILE, TILE), TILE)
            if array == 0:
                term = jnp.dot(xs[o, 0:LIVE, :], win_buf[slot, :, cols], preferred_element_type=f32)
                if k == 0:
                    pre[:, cols] = term + bias_ref[:, cols].astype(f32)
                else:
                    pre[:, cols] += term
            else:
                term = lax.dot_general(
                    dys[o], wout_buf[slot, cols, :], (((1,), (1,)), ((), ())), preferred_element_type=f32
                )
                if k == 0:
                    back[:, cols] = term
                elif k < 7:
                    back[:, cols] += term
                else:
                    dpre = ((back[:, cols] + term) * pre[:, cols]).astype(bf16)
                    part = jnp.dot(dpre, proj_buf[cols, :], preferred_element_type=f32)
                    right[...] += part

    for array in range(2):
        for k in range(8):
            if array == 0 and k == 6:
                pass_on(1, 0)
            if k == 1:
                pass_on(array, 1, 2)
                pl.when(rank == 1)(functools.partial(pass_on, array, 3))
            elif k == 3:
                pl.when(rank == 0)(functools.partial(pass_on, array, 3))
            elif k > 3:
                pass_on(array, k)
            if array == 0 and k == 7:
                own = maps.at[group]
                for peer in range(1, 4):
                    pltpu.make_async_remote_copy(
                        src_ref=xs.at[:, pl.ds(LIVE, SHARE), :],
                        dst_ref=own,
                        send_sem=map_send.at[peer],
                        recv_sem=map_recv.at[peer],
                        device_id={"query": (q + peer // 2) % 2, "ckpt": (c + peer % 2) % 2},
                        device_id_type=pl.DeviceIdType.MESH,
                    ).start()
                maps[group] = xs[:, LIVE : LIVE + SHARE, :]
            ahead = array * 8 + k + 2
            if ahead < 16:
                weights(ahead // 8, ahead % 8).start()
            weights(array, k).wait()
            accumulate(array, k)
            if array == 1 and k in (0, 2, 3, 4):
                first = (0, 0, tiles - 3, tiles - 2, tiles - 1)[k]
                for t in range(first, first + 1 if k else tiles - 3):
                    cols = pl.ds(t * TILE, TILE)
                    pre[:, cols] = gelu_slope_tile(pre[:, cols])
            if array == 1 and k == 5:
                right[...] = jnp.zeros_like(right)
                for peer in range(1, 4):
                    other = ((q + peer // 2) % 2) * 2 + (c + peer % 2) % 2
                    pltpu.make_async_remote_copy(
                        src_ref=xs.at[:, pl.ds(LIVE, SHARE), :],
                        dst_ref=maps.at[other],
                        send_sem=map_send.at[peer],
                        recv_sem=map_recv.at[peer],
                        device_id={"query": (q + peer // 2) % 2, "ckpt": (c + peer % 2) % 2},
                        device_id_type=pl.DeviceIdType.MESH,
                    ).wait()
                left = jnp.zeros((LIVE, k_in), f32)
                for o in range(8):
                    left += lax.dot_general(
                        xs[o, 0:LIVE, :],
                        maps[:, o].reshape(k_in, width),
                        (((1,), (1,)), ((), ())),
                        preferred_element_type=f32,
                    )
                gram[...] = lax.dot_general(
                    left, left, (((1,), (1,)), ((), ())), precision=HIGH, preferred_element_type=f32
                )
                all_sent(0)

    token = lax.broadcasted_iota(jnp.int32, (LIVE, 64), 0).astype(f32)
    start, size = spans(64, lambda t: jnp.where(t % 8 < 4, t // 8 * 4 + t % 8, -1))
    train = jnp.where((token >= start) & (token < start + size), 1.0, 0.0)
    token = lax.broadcasted_iota(jnp.int32, (LIVE, 128), 0).astype(f32)
    start, size = spans(128, lambda t: t + NTR)
    test = jnp.where((token >= start) & (token < start + size), 1.0, 0.0)

    parts_out[...] = right[...].T.reshape(8, k_out // 8, LIVE)

    def part_copy(d):
        return pltpu.make_async_remote_copy(
            src_ref=parts_out.at[(me + d) % 8],
            dst_ref=parts_in.at[d],
            send_sem=part_send.at[d],
            recv_sem=part_recv.at[d],
            device_id={"mp": (me + d) % 8},
            device_id_type=pl.DeviceIdType.MESH,
        )

    for d in range(1, 8):
        part_copy(d).start()
    parts_in[0] = parts_out[me]
    all_sent(1)
    for d in range(1, 8):
        part_copy(d).wait_recv()
    total = jnp.sum(parts_in[...], axis=0)
    both = gram[...] * jnp.dot(total.T, total, precision=HIGH, preferred_element_type=f32)
    half = jnp.dot(both, test, precision=HIGH, preferred_element_type=f32)
    score = jnp.dot(train.T, half, precision=HIGH, preferred_element_type=f32)
    score = score * (rate_ref[0] / math.sqrt(k_in * k_out))
    tile_out[...] = score.reshape(8, 8, 128)

    def tile_copy(d, dc):
        return pltpu.make_async_remote_copy(
            src_ref=tile_out.at[(me + d) % 8],
            dst_ref=tile_in.at[d * 2 + dc],
            send_sem=tile_send.at[d * 2 + dc],
            recv_sem=tile_recv.at[d * 2 + dc],
            device_id={"mp": (me + d) % 8, "ckpt": (c + dc) % 2},
            device_id_type=pl.DeviceIdType.MESH,
        )

    for d in range(8):
        for dc in range(2):
            if d or dc:
                tile_copy(d, dc).start()
    tile_in[0] = tile_out[me]
    for d in range(1, 8):
        part_copy(d).wait_send()
    for d in range(8):
        for dc in range(2):
            if d or dc:
                tile_copy(d, dc).wait()
    out_ref[...] = jnp.sum(tile_in[...], axis=0)[0:4, 0:8]


def gelu_slope_tile(z):
    return 0.5 * (1.0 + lax.erf(z * (1.0 / math.sqrt(2.0)))) + z * jnp.exp(-0.5 * z * z) * (
        1.0 / math.sqrt(2.0 * math.pi)
    )


def fused(activations, cotangents, w_in, b_in, w_out, rates, proj_in, proj_out, lengths):
    width = activations.shape[2]
    hidden = w_in.shape[2]
    k_in = proj_in.shape[0]
    k_out = proj_out.shape[1]
    f32, bf16 = jnp.float32, jnp.bfloat16
    vmem = pl.BlockSpec(memory_space=pltpu.VMEM)
    hbm = pl.BlockSpec(memory_space=pl.ANY)
    smem = pl.BlockSpec(memory_space=pltpu.SMEM)
    dma = pltpu.SemaphoreType.DMA
    return pl.pallas_call(
        fused_kernel,
        out_shape=jax.ShapeDtypeStruct((4, 8), f32),
        in_specs=[vmem, hbm, hbm, vmem, hbm, smem, vmem, hbm, vmem],
        out_specs=vmem,
        scratch_shapes=[
            pltpu.VMEM((8, LIVE + SHARE, width), bf16),
            pltpu.VMEM((8, LIVE, width), bf16),
            pltpu.VMEM((3, width, hidden), bf16),
            pltpu.VMEM((3, hidden, width), bf16),
            pltpu.VMEM((LIVE, hidden), f32),
            pltpu.VMEM((LIVE, hidden), f32),
            pltpu.VMEM((4, 8, SHARE, width), bf16),
            pltpu.VMEM((LIVE, k_out), f32),
            pltpu.VMEM((LIVE, LIVE), f32),
            pltpu.VMEM((8, k_out // 8, LIVE), f32),
            pltpu.VMEM((8, k_out // 8, LIVE), f32),
            pltpu.VMEM((8, 8, 128), f32),
            pltpu.VMEM((16, 8, 128), f32),
            pltpu.VMEM(cotangents.shape[1:], bf16),
            pltpu.VMEM(proj_out.shape, bf16),
            dma((2,)),
            dma((2, 8, PARTS, 3)),
            dma((2, 8, PARTS)),
            dma((2, 3)),
            dma((4,)),
            dma((4,)),
            dma((8,)),
            dma((8,)),
            dma((16,)),
            dma((16,)),
        ],
        compiler_params=pltpu.CompilerParams(
            collective_id=0, has_side_effects=True, vmem_limit_bytes=60 * 1024 * 1024
        ),
        cost_estimate=pl.CostEstimate(
            flops=4 * LIVE * 8 * width * hidden,
            bytes_accessed=32 * width * hidden,
            transcendentals=2 * LIVE * hidden,
        ),
        name="influence",
    )(
        activations, cotangents, w_in, b_in, w_out, rates, proj_in, proj_out,
        lengths.reshape(1, lengths.shape[0]),
    )


def solution(mesh):
    placed = (
        P("ckpt", "query", "mp"),
        P("ckpt", "query", "mp"),
        P("ckpt", None, "mp"),
        P("ckpt", "mp"),
        P("ckpt", "mp", None),
        P("ckpt"),
        P(None, "mp"),
        P("mp", None),
        P("query"),
    )
    fits = mesh.shape["mp"] == 8 and mesh.shape["query"] == 2 and mesh.shape["ckpt"] == 2
    return jax.shard_map(
        fused if fits else body,
        mesh=mesh,
        in_specs=placed,
        out_specs=P(("query", "mp"), None),
        check_vma=False,
    )
```

```python
import functools
import math

import jax
import jax.numpy as jnp
from jax import lax
from jax.experimental import pallas as pl
from jax.experimental.pallas import tpu as pltpu
from jax.sharding import PartitionSpec as P

NTR = 32
LIVE = 400


def gelu_slope(z):
    return 0.5 * (1.0 + jax.scipy.special.erf(z / math.sqrt(2.0))) + z * jnp.exp(
        -0.5 * z * z
    ) / math.sqrt(2.0 * math.pi)


def body(activations, cotangents, w_in, b_in, w_out, rates, proj_in, proj_out, lengths):
    x_local = activations[0]
    dy_local = cotangents[0]
    w_first = w_in[0]
    w_second = w_out[0]
    bias = b_in[0]
    rate = rates[0]
    examples = lengths.shape[0]
    padded_rows = x_local.shape[0]
    seq = padded_rows // examples
    k_in = proj_in.shape[0]
    k_out = proj_out.shape[1]
    columns = jnp.arange(examples, dtype=jnp.int32)
    ends = jnp.cumsum(lengths)
    starts = ends - lengths
    row_ids = jnp.arange(LIVE, dtype=jnp.int32)
    owner = jnp.sum((row_ids[:, None] >= ends[None, :]).astype(jnp.int32), axis=1)
    belongs = owner[:, None] == columns[None, :]
    start_of = jnp.sum(jnp.where(belongs, starts[None, :], 0), axis=1)
    source = owner * seq + row_ids - start_of
    x_rows = jnp.take(x_local, source, axis=0)
    dy_rows = jnp.take(dy_local, source, axis=0)
    live = jnp.ones((LIVE,), jnp.float32)

    def to_slots(values):
        slots = jnp.zeros((padded_rows, values.shape[1]), jnp.float32).at[source].set(values)
        return slots.reshape(examples, seq, values.shape[1])

    x_piece = lax.all_gather(x_rows, "mp", axis=1, tiled=True)
    map_piece = lax.all_gather(proj_in, "mp", axis=1, tiled=True)
    pre_acc = jnp.dot(x_piece, w_first, preferred_element_type=jnp.float32)
    left_acc = lax.dot_general(
        x_piece, map_piece, (((1,), (1,)), ((), ())), preferred_element_type=jnp.float32
    )
    pre = pre_acc
    left = left_acc
    pre = pre + bias.astype(jnp.float32)
    back = lax.dot_general(
        lax.all_gather(dy_rows, "mp", axis=1, tiled=True),
        w_second,
        (((1,), (1,)), ((), ())),
        preferred_element_type=jnp.float32,
    )
    dpre = (back * gelu_slope(pre)).astype(jnp.bfloat16)
    left = left * live[:, None]
    right = jnp.dot(dpre, proj_out, preferred_element_type=jnp.float32)
    factor = rate / math.sqrt(k_in * k_out)
    left_blocks = to_slots(left)
    right_blocks = to_slots(right)
    grads = jnp.einsum("esi,esj->ije", left_blocks, right_blocks, precision=lax.Precision.HIGHEST)
    grads = grads.reshape(k_in * k_out, examples)
    owned = lax.psum_scatter(grads, "mp", scatter_dimension=0, tiled=True)
    partial_tile = (
        lax.dot_general(
            owned[:, :NTR],
            owned[:, NTR:],
            (((0,), (0,)), ((), ())),
            precision=lax.Precision.HIGHEST,
        )
        * factor
    )
    tile = lax.psum_scatter(partial_tile, "mp", scatter_dimension=0, tiled=True)
    return lax.psum(tile, "ckpt")


PIECES = (
    ((0, 1), (1, 1), (0, 0), (2, 1), (2, 0), (3, 1), (3, 0), (1, 0)),
    ((1, 1), (2, 1), (1, 0), (0, 1), (3, 1), (0, 0), (2, 0), (3, 0)),
)
INWARD, OUTWARD, ACROSS = 0, 1, 2
TILE = 512
SHARE = 16
HIGH = lax.Precision.HIGHEST
PARTS = 4


def routes(rank, owner, same, part):
    out = []
    if same:
        if owner <= rank:
            out.append(INWARD)
        if rank == 1 and owner >= 1:
            out.append(OUTWARD)
        if rank == 0 and not (owner == 1 and part >= PARTS // 2):
            out.append(ACROSS)
        if rank == 1 and owner != 0:
            out.append(ACROSS)
    elif rank == 0 and owner == 0:
        out.append(INWARD)
    return out


def fused_kernel(
    x_ref, dy_ref, w_in, bias_ref, w_out, rate_ref, map_ref, proj_ref, len_ref,
    out_ref,
    xs, dys, win_buf, wout_buf, pre, back, maps, right, gram, parts_out, parts_in, tile_out, tile_in, dy_buf, proj_buf, train, test,
    load_sem, send_sem, recv_sem, w_sem, map_send, map_recv, part_send, part_recv, tile_send, tile_recv,
):
    f32, bf16 = jnp.float32, jnp.bfloat16
    me = lax.axis_index("mp")
    q = lax.axis_index("query")
    c = lax.axis_index("ckpt")
    z = me // 2
    y = me % 2
    far = z // 2
    rank = z + far * (3 - 2 * z)
    group = q * 2 + c
    width = x_ref.shape[2]
    hidden = w_in.shape[2]
    tiles = hidden // TILE
    examples = len_ref.shape[1]
    padded = x_ref.shape[1]
    seq = padded // examples
    last = gram.shape[1]
    k_in = map_ref.shape[0]
    k_out = proj_ref.shape[1]
    stacks = (xs, dys)
    cuts = []
    for stack in stacks:
        blocks = stack.shape[1] // SHARE
        edges = [blocks * p // PARTS * SHARE for p in range(PARTS + 1)]
        cuts.append([(a, b - a) for a, b in zip(edges, edges[1:])])

    barrier = pltpu.get_barrier_semaphore()
    for d in range(16):
        for dc in range(2):
            if d < 8 and (d or dc):
                pl.semaphore_signal(
                    barrier, inc=1,
                    device_id={"mp": (me + d) % 8, "ckpt": (c + dc) % 2},
                    device_id_type=pl.DeviceIdType.MESH,
                )
    for dc in range(2):
        pl.semaphore_signal(
            barrier, inc=1,
            device_id={"query": 1 - q, "ckpt": (c + dc) % 2},
            device_id_type=pl.DeviceIdType.MESH,
        )

    def index_of(owner, same):
        zz = owner + far * (3 - 2 * owner)
        return zz * 2 + (y + 1 - same) % 2

    def piece(k):
        (o0, s0), (o1, s1) = PIECES[0][k], PIECES[1][k]
        return index_of(o0 + rank * (o1 - o0), s0 + rank * (s1 - s0))

    def weights(array, k):
        slot = (array * 8 + k) % 3
        at = pl.multiple_of(piece(k) * width, 128)
        if array == 0:
            return pltpu.make_async_copy(
                w_in.at[0, pl.ds(at, width), :], win_buf.at[slot], w_sem.at[array, slot]
            )
        return pltpu.make_async_copy(
            w_out.at[0, :, pl.ds(at, width)], wout_buf.at[slot], w_sem.at[array, slot]
        )

    dy_load = pltpu.make_async_copy(dy_ref.at[0], dy_buf, load_sem.at[0])
    proj_load = pltpu.make_async_copy(proj_ref, proj_buf, load_sem.at[1])
    dy_load.start()
    proj_load.start()
    for k in range(2):
        weights(0, k).start()

    lens = jnp.broadcast_to(len_ref[...].astype(f32), (8, examples)).astype(bf16)

    def spans(count, example_of):
        e = lax.broadcasted_iota(jnp.int32, (examples, count), 0)
        t = example_of(lax.broadcasted_iota(jnp.int32, (examples, count), 1))
        start = jnp.dot(lens, (e < t).astype(f32).astype(bf16), preferred_element_type=f32)
        size = jnp.dot(lens, (e == t).astype(f32).astype(bf16), preferred_element_type=f32)
        return start[0:1], size[0:1]

    start, size = spans(padded, lambda t: t // seq)
    place = (lax.broadcasted_iota(jnp.int32, (1, padded), 1) % seq).astype(f32)
    target = jnp.where(place < size, start + place, -1.0)
    rows = lax.broadcasted_iota(jnp.int32, (LIVE, padded), 0).astype(f32)
    pick = jnp.where(rows == target, 1.0, 0.0).astype(bf16)
    xs[me, 0:LIVE, :] = jnp.dot(pick, x_ref[0], preferred_element_type=f32).astype(bf16)
    xs[me, LIVE : LIVE + SHARE, :] = map_ref[pl.ds(pl.multiple_of(group * SHARE, SHARE), SHARE), :]

    pl.semaphore_wait(barrier, 17)

    sgn = 1 - 2 * far
    targets = ((z + sgn) * 2 + y, (z - sgn) * 2 + y, z * 2 + 1 - y)

    def copy(array, k, part, direction):
        o = piece(k)
        first, count = cuts[array][part]
        there = stacks[array].at[o, pl.ds(first, count), :]
        return pltpu.make_async_remote_copy(
            src_ref=there,
            dst_ref=there,
            send_sem=send_sem.at[array, k, part, direction],
            recv_sem=recv_sem.at[array, o, part],
            device_id={"mp": targets[direction]},
            device_id_type=pl.DeviceIdType.MESH,
        )

    def each_route(array, k, part, do):
        for direction in (OUTWARD, INWARD, ACROSS):
            ranks = [r for r in range(2) if direction in routes(r, *PIECES[r][k], part)]
            if len(ranks) == 2:
                do(array, k, part, direction)
            elif ranks:
                pl.when(rank == ranks[0])(functools.partial(do, array, k, part, direction))
        if k == 4 and part >= PARTS // 2:
            pl.when(rank == 1)(functools.partial(do, array, 2, part, OUTWARD))

    def send(array, k, part, direction):
        copy(array, k, part, direction).start()

    def sent(array, k, part, direction):
        copy(array, k, part, direction).wait_send()

    def pass_on(array, *ks):
        for part in range(PARTS):
            for k in ks:
                if k > 0:
                    copy(array, k, part, ACROSS).wait_recv()
                each_route(array, k, part, send)

    def all_sent(array):
        for k in range(8):
            for part in range(PARTS):
                each_route(array, k, part, sent)

    pass_on(0, 0)
    dy_load.wait()
    proj_load.wait()
    dys[me] = jnp.dot(pick, dy_buf[...], preferred_element_type=f32).astype(bf16)

    def accumulate(array, k):
        o = piece(k)
        slot = (array * 8 + k) % 3

        @pl.loop(0, tiles)
        def _(t):
            cols = pl.ds(pl.multiple_of(t * TILE, TILE), TILE)
            if array == 0:
                term = jnp.dot(xs[o, 0:LIVE, :], win_buf[slot, :, cols], preferred_element_type=f32)
                if k == 0:
                    pre[:, cols] = term + bias_ref[:, cols].astype(f32)
                else:
                    pre[:, cols] += term
            else:
                term = lax.dot_general(
                    dys[o], wout_buf[slot, cols, :], (((1,), (1,)), ((), ())), preferred_element_type=f32
                )
                if k == 0:
                    back[:, cols] = term
                elif k < 7:
                    back[:, cols] += term
                else:
                    dpre = ((back[:, cols] + term) * pre[:, cols]).astype(bf16)
                    part = jnp.dot(dpre, proj_buf[cols, :], preferred_element_type=f32)
                    right[...] += part

    for array in range(2):
        for k in range(8):
            if array == 0 and k == 6:
                pass_on(1, 0)
            if k == 1:
                pass_on(array, 1, 2)
                pl.when(rank == 1)(functools.partial(pass_on, array, 3))
            elif k == 3:
                pl.when(rank == 0)(functools.partial(pass_on, array, 3))
            elif k > 3:
                pass_on(array, k)
            if array == 0 and k == 7:
                own = maps.at[group]
                for peer in range(1, 4):
                    pltpu.make_async_remote_copy(
                        src_ref=xs.at[:, pl.ds(LIVE, SHARE), :],
                        dst_ref=own,
                        send_sem=map_send.at[peer],
                        recv_sem=map_recv.at[peer],
                        device_id={"query": (q + peer // 2) % 2, "ckpt": (c + peer % 2) % 2},
                        device_id_type=pl.DeviceIdType.MESH,
                    ).start()
                maps[group] = xs[:, LIVE : LIVE + SHARE, :]
            ahead = array * 8 + k + 2
            if ahead < 16:
                weights(ahead // 8, ahead % 8).start()
            weights(array, k).wait()
            accumulate(array, k)
            if array == 1 and k in (0, 2, 3, 4):
                first = (0, 0, tiles - 3, tiles - 2, tiles - 1)[k]
                for t in range(first, first + 1 if k else tiles - 3):
                    cols = pl.ds(t * TILE, TILE)
                    pre[:, cols] = gelu_slope_tile(pre[:, cols])
            if array == 1 and k == 5:
                right[...] = jnp.zeros_like(right)
                for peer in range(1, 4):
                    other = ((q + peer // 2) % 2) * 2 + (c + peer % 2) % 2
                    pltpu.make_async_remote_copy(
                        src_ref=xs.at[:, pl.ds(LIVE, SHARE), :],
                        dst_ref=maps.at[other],
                        send_sem=map_send.at[peer],
                        recv_sem=map_recv.at[peer],
                        device_id={"query": (q + peer // 2) % 2, "ckpt": (c + peer % 2) % 2},
                        device_id_type=pl.DeviceIdType.MESH,
                    ).wait()
                left = jnp.zeros((LIVE, k_in), f32)
                for o in range(8):
                    left += lax.dot_general(
                        xs[o, 0:LIVE, :],
                        maps[:, o].reshape(k_in, width),
                        (((1,), (1,)), ((), ())),
                        preferred_element_type=f32,
                    )
                first = LIVE - last
                gram[...] = lax.dot_general(
                    left, left[first:], (((1,), (1,)), ((), ())), precision=HIGH, preferred_element_type=f32
                )
                token = lax.broadcasted_iota(jnp.int32, (LIVE, 64), 0).astype(f32)
                start, size = spans(64, lambda t: jnp.where(t % 8 < 4, t // 8 * 4 + t % 8, -1))
                train[...] = jnp.where((token >= start) & (token < start + size), 1.0, 0.0).T
                token = lax.broadcasted_iota(jnp.int32, (last, 128), 0).astype(f32) + first
                start, size = spans(128, lambda t: t + NTR)
                test[...] = jnp.where((token >= start) & (token < start + size), 1.0, 0.0)
                all_sent(0)

    parts_out[...] = right[...].T.reshape(8, k_out // 8, LIVE)

    def part_copy(d):
        return pltpu.make_async_remote_copy(
            src_ref=parts_out.at[(me + d) % 8],
            dst_ref=parts_in.at[d],
            send_sem=part_send.at[d],
            recv_sem=part_recv.at[d],
            device_id={"mp": (me + d) % 8},
            device_id_type=pl.DeviceIdType.MESH,
        )

    for d in range(1, 8):
        part_copy(d).start()
    parts_in[0] = parts_out[me]
    all_sent(1)
    for d in range(1, 8):
        part_copy(d).wait_recv()
    total = jnp.sum(parts_in[...], axis=0)
    total = total.T
    both = gram[...] * lax.dot_general(
        total, total[LIVE - last :], (((1,), (1,)), ((), ())), precision=HIGH, preferred_element_type=f32
    )
    half = jnp.dot(both, test[...], precision=HIGH, preferred_element_type=f32)
    score = jnp.dot(train[...], half, precision=HIGH, preferred_element_type=f32)
    score = score * (rate_ref[0] / math.sqrt(k_in * k_out))
    tile_out[...] = score.reshape(8, 8, 128)

    def tile_copy(d, dc):
        return pltpu.make_async_remote_copy(
            src_ref=tile_out.at[(me + d) % 8],
            dst_ref=tile_in.at[d * 2 + dc],
            send_sem=tile_send.at[d * 2 + dc],
            recv_sem=tile_recv.at[d * 2 + dc],
            device_id={"mp": (me + d) % 8, "ckpt": (c + dc) % 2},
            device_id_type=pl.DeviceIdType.MESH,
        )

    for d in range(8):
        for dc in range(2):
            if d or dc:
                tile_copy(d, dc).start()
    tile_in[0] = tile_out[me]
    for d in range(1, 8):
        part_copy(d).wait_send()
    for d in range(8):
        for dc in range(2):
            if d or dc:
                tile_copy(d, dc).wait()
    out_ref[...] = jnp.sum(tile_in[...], axis=0)[0:4, 0:8]


def gelu_slope_tile(z):
    return 0.5 * (1.0 + lax.erf(z * (1.0 / math.sqrt(2.0)))) + z * jnp.exp(-0.5 * z * z) * (
        1.0 / math.sqrt(2.0 * math.pi)
    )


def fused(activations, cotangents, w_in, b_in, w_out, rates, proj_in, proj_out, lengths):
    width = activations.shape[2]
    hidden = w_in.shape[2]
    k_in = proj_in.shape[0]
    k_out = proj_out.shape[1]
    examples = lengths.shape[0]
    last = activations.shape[1] // examples * (examples - NTR)
    f32, bf16 = jnp.float32, jnp.bfloat16
    vmem = pl.BlockSpec(memory_space=pltpu.VMEM)
    hbm = pl.BlockSpec(memory_space=pl.ANY)
    smem = pl.BlockSpec(memory_space=pltpu.SMEM)
    dma = pltpu.SemaphoreType.DMA
    return pl.pallas_call(
        fused_kernel,
        out_shape=jax.ShapeDtypeStruct((4, 8), f32),
        in_specs=[vmem, hbm, hbm, vmem, hbm, smem, vmem, hbm, vmem],
        out_specs=vmem,
        scratch_shapes=[
            pltpu.VMEM((8, LIVE + SHARE, width), bf16),
            pltpu.VMEM((8, LIVE, width), bf16),
            pltpu.VMEM((3, width, hidden), bf16),
            pltpu.VMEM((3, hidden, width), bf16),
            pltpu.VMEM((LIVE, hidden), f32),
            pltpu.VMEM((LIVE, hidden), f32),
            pltpu.VMEM((4, 8, SHARE, width), bf16),
            pltpu.VMEM((LIVE, k_out), f32),
            pltpu.VMEM((LIVE, last), f32),
            pltpu.VMEM((8, k_out // 8, LIVE), f32),
            pltpu.VMEM((8, k_out // 8, LIVE), f32),
            pltpu.VMEM((8, 8, 128), f32),
            pltpu.VMEM((16, 8, 128), f32),
            pltpu.VMEM(cotangents.shape[1:], bf16),
            pltpu.VMEM(proj_out.shape, bf16),
            pltpu.VMEM((64, LIVE), f32),
            pltpu.VMEM((last, 128), f32),
            dma((2,)),
            dma((2, 8, PARTS, 3)),
            dma((2, 8, PARTS)),
            dma((2, 3)),
            dma((4,)),
            dma((4,)),
            dma((8,)),
            dma((8,)),
            dma((16,)),
            dma((16,)),
        ],
        compiler_params=pltpu.CompilerParams(
            collective_id=0, has_side_effects=True, vmem_limit_bytes=60 * 1024 * 1024
        ),
        cost_estimate=pl.CostEstimate(
            flops=4 * LIVE * 8 * width * hidden,
            bytes_accessed=32 * width * hidden,
            transcendentals=2 * LIVE * hidden,
        ),
        name="influence",
    )(
        activations, cotangents, w_in, b_in, w_out, rates, proj_in, proj_out,
        lengths.reshape(1, lengths.shape[0]),
    )


def solution(mesh):
    placed = (
        P("ckpt", "query", "mp"),
        P("ckpt", "query", "mp"),
        P("ckpt", None, "mp"),
        P("ckpt", "mp"),
        P("ckpt", "mp", None),
        P("ckpt"),
        P(None, "mp"),
        P("mp", None),
        P("query"),
    )
    fits = mesh.shape["mp"] == 8 and mesh.shape["query"] == 2 and mesh.shape["ckpt"] == 2
    return jax.shard_map(
        fused if fits else body,
        mesh=mesh,
        in_specs=placed,
        out_specs=P(("query", "mp"), None),
        check_vma=False,
    )
```
